128 devices in a mesh: wide: 64 (over z, y_hi, x, core), narrow: 2 (over y_lo).
Axes of the slice: x: 4, y: 4 (y_hi: 2, y_lo: 2; y = y_hi * 2 + y_lo), z: 4, core: 2. Of those that a mesh axis runs over, the one named last changes fastest.
Arguments:
- tokens: bfloat16 [128, 256, 512], P('wide', 'narrow'), may hold values from -6 to 6
- captions: bfloat16 [128, 128, 768], P('wide'), may hold values from -6 to 6
- caption_len: int32 [128], P('wide'), may hold values from 8 to 128, as said below
- timestep: int32 [128], P('wide'), may hold values from 0 to 999
- time_table: float32 [1000, 512], replicated, may hold values from -6 to 6
- cotangent: bfloat16 [128, 256, 512], P('wide', 'narrow'), may hold values from -6 to 6
- w_ada: float32 [512, 3072], P('wide'), may hold values from -0.25 to 0.25
- w_qkv: float32 [512, 1536], P('wide'), may hold values from -0.375 to 0.375
- w_out: float32 [512, 512], P('wide'), may hold values from -0.75 to 0.75
- w_cq: float32 [512, 512], P('wide'), may hold values from -0.375 to 0.375
- w_ckv: float32 [768, 1024], P('wide'), may hold values from -0.3125 to 0.3125
- w_cout: float32 [512, 512], P('wide'), may hold values from -0.5 to 0.5
- w_up: float32 [512, 2048], P('wide'), may hold values from -0.25 to 0.25
- w_down: float32 [2048, 512], P('wide'), may hold values from -0.125 to 0.125
- m_ada: float32 [512, 3072], P('wide'), may hold values from -512 to 512
- m_qkv: float32 [512, 1536], P('wide'), may hold values from -1024 to 1024
- m_out: float32 [512, 512], P('wide'), may hold values from -512 to 512
- m_cq: float32 [512, 512], P('wide'), may hold values from -512 to 512
- m_ckv: float32 [768, 1024], P('wide'), may hold values from -512 to 512
- m_cout: float32 [512, 512], P('wide'), may hold values from -512 to 512
- m_up: float32 [512, 2048], P('wide'), may hold values from -512 to 512
- m_down: float32 [2048, 512], P('wide'), may hold values from -512 to 512
Outputs:
- output: bfloat16 [128, 256, 512], P('wide', 'narrow')
- grad_tokens: float32 [128, 256, 512], P('wide', 'narrow')
- grad_captions: float32 [128, 128, 768], P('wide', 'narrow')
- new_m_ada: float32 [512, 3072], P('wide')
- new_m_qkv: float32 [512, 1536], P('wide')
- new_m_out: float32 [512, 512], P('wide')
- new_m_cq: float32 [512, 512], P('wide')
- new_m_ckv: float32 [768, 1024], P('wide')
- new_m_cout: float32 [512, 512], P('wide')
- new_m_up: float32 [512, 2048], P('wide')
- new_m_down: float32 [2048, 512], P('wide')
- new_w_ada: float32 [512, 3072], P('wide')
- new_w_qkv: float32 [512, 1536], P('wide')
- new_w_out: float32 [512, 512], P('wide')
- new_w_cq: float32 [512, 512], P('wide')
- new_w_ckv: float32 [768, 1024], P('wide')
- new_w_cout: float32 [512, 512], P('wide')
- new_w_up: float32 [512, 2048], P('wide')
- new_w_down: float32 [2048, 512], P('wide')
The draws below stay inside these ranges and needn't reach their ends.
Inputs may be any that keep to these rules, and one draw needn't show every extreme that they name: `caption_len`: each image has at least 8 live caption tokens; in every draw some image has all 128.
All inputs are finite; a program needn't handle non-finite values.
Results may differ from the reference program's by a relative error of at most 0.025.
The reference program's roundings to bfloat16 on the way count: a program that leaves them out, or rounds other values in their place, can miss the bound.
Values may be sent and summed in bfloat16 or wider, within the bound.
No kernel may reach another device: no remote copies, remote signals or barrier semaphores. Data moves between devices by JAX's collectives and lax.ppermute only.
A program may use at most 192 MiB of HBM per device.

```python
import math
import jax
import jax.numpy as jnp
from jax import lax

D = 512
HEADS = 8
HEAD = 64
FF = 2048
TD = 768
TLEN = 128
SEQ = 256
NSTEPS = 1000
NEWTON_STEPS = 5
IMAGES = 128


def draw_caption_len(key, part):
    key = jax.random.fold_in(key, 7)
    first_key, second_key = jax.random.split(key)
    drawn = jax.random.randint(first_key, (IMAGES,), 8, TLEN + 1)
    chosen = jax.random.randint(second_key, (), 0, IMAGES)
    return jnp.where(jnp.arange(IMAGES) == chosen, TLEN, drawn).astype(jnp.int32)


def place_ends(values, rng, smallest, top_value):
    shape = values.shape
    place = [jax.random.randint(jax.random.fold_in(rng, axis), (), 0, shape[axis]) for axis in range(len(shape))]
    values = values.at[tuple(place)].set(smallest)
    longest = shape.index(max(shape))
    place[longest] = (place[longest] + 1) % shape[longest]
    return values.at[tuple(place)].set(top_value)


def level_of(key, dims, shards, low, high):
    factor_of, own = 1.0, jax.random.fold_in(key, 6)
    for dim, blocks in shards:
        draws = jnp.exp(jax.random.uniform(jax.random.fold_in(own, dim), (blocks,), jnp.float32, low / len(shards), high / len(shards)))
        factor_of = factor_of * jnp.repeat(draws, dims[dim] // blocks).reshape([-1 if axis == dim else 1 for axis in range(len(dims))])
    return factor_of


def gaussian(own_key, extent, scale, reach, pieces=(), held_as=jnp.bfloat16):
    values = jax.random.normal(own_key, extent, jnp.float32) * scale
    if len(pieces) > 0:
        values = level_of(own_key, extent, pieces, -0.22, 0.18) * values
    return jnp.clip(values, min=-reach, max=reach).astype(held_as)


def setup_inputs(seed: int = 0) -> dict:
    key_of = jax.random.split(jax.random.key(seed), 23)
    return {
        "tokens": gaussian(key_of[0], (IMAGES, SEQ, D), 1.0, 6.0, ((0, 64), (1, 2))),
        "captions": gaussian(key_of[1], (IMAGES, TLEN, TD), 1.0, 6.0, ((0, 64),)),
        "caption_len": draw_caption_len(jax.random.fold_in(key_of[22], 71), 0),
        "timestep": place_ends(jax.random.randint(key_of[3], (IMAGES,), 0, NSTEPS), jax.random.fold_in(key_of[3], 1), 0, NSTEPS - 1).astype(jnp.int32),
        "time_table": gaussian(key_of[4], (NSTEPS, D), 1.0, 6.0, (), jnp.float32),
        "cotangent": gaussian(key_of[5], (IMAGES, SEQ, D), 1.0, 6.0, ((0, 64), (1, 2))),
        "w_ada": gaussian(key_of[6], (D, 6 * D), D ** -0.5, 0.25, ((0, 64),), jnp.float32),
        "w_qkv": gaussian(key_of[7], (D, 3 * D), (D // 2) ** -0.5, 0.375, ((0, 64),), jnp.float32),
        "w_out": gaussian(key_of[8], (D, D), (D // 8) ** -0.5, 0.75, ((0, 64),), jnp.float32),
        "w_cq": gaussian(key_of[9], (D, D), (D // 2) ** -0.5, 0.375, ((0, 64),), jnp.float32),
        "w_ckv": gaussian(key_of[10], (TD, 2 * D), (TD // 2) ** -0.5, 0.3125, ((0, 64),), jnp.float32),
        "w_cout": gaussian(key_of[11], (D, D), (D // 4) ** -0.5, 0.5, ((0, 64),), jnp.float32),
        "w_up": gaussian(key_of[12], (D, FF), D ** -0.5, 0.25, ((0, 64),), jnp.float32),
        "w_down": gaussian(key_of[13], (FF, D), FF ** -0.5, 0.125, ((0, 64),), jnp.float32),
        "m_ada": gaussian(key_of[14], (D, 6 * D), (0.5 * (IMAGES * SEQ) ** 0.5), 512.0, ((0, 64),), jnp.float32),
        "m_qkv": gaussian(key_of[15], (D, 3 * D), (1.0 * (IMAGES * SEQ) ** 0.5), 1024.0, ((0, 64),), jnp.float32),
        "m_out": gaussian(key_of[16], (D, D), (0.5 * (IMAGES * SEQ) ** 0.5), 512.0, ((0, 64),), jnp.float32),
        "m_cq": gaussian(key_of[17], (D, D), (0.5 * (IMAGES * SEQ) ** 0.5), 512.0, ((0, 64),), jnp.float32),
        "m_ckv": gaussian(key_of[18], (TD, 2 * D), (0.5 * (IMAGES * SEQ) ** 0.5), 512.0, ((0, 64),), jnp.float32),
        "m_cout": gaussian(key_of[19], (D, D), (0.5 * (IMAGES * SEQ) ** 0.5), 512.0, ((0, 64),), jnp.float32),
        "m_up": gaussian(key_of[20], (D, FF), (0.5 * (IMAGES * SEQ) ** 0.5), 512.0, ((0, 64),), jnp.float32),
        "m_down": gaussian(key_of[21], (FF, D), (0.5 * (IMAGES * SEQ) ** 0.5), 512.0, ((0, 64),), jnp.float32),
    }


@jax.custom_vjp
def low(v):
    return lax.optimization_barrier(v.astype(jnp.bfloat16)).astype(jnp.float32)

@jax.custom_vjp
def low_back(v):
    return v

def low_keep(v):
    return (low(v), None)

def low_pass(kept, grad):
    return (grad,)

def back_keep(v):
    return (v, None)

def back_low(kept, grad):
    return (low(grad),)
low.defvjp(low_keep, low_pass)
low_back.defvjp(back_keep, back_low)
EPSILON = 1e-06
MASKED = -1e+30
RATE = 1.0
DECAY = 0.5
COEF_A = 3.4445
COEF_B = -4.775
COEF_C = 2.0315

def matmul(left, right):
    return jnp.dot(left, right, precision=lax.Precision.HIGHEST, preferred_element_type=jnp.float32)

def layer_norm(signal):
    centre = lax.optimization_barrier(jnp.mean(signal, axis=-1, keepdims=True))
    centred = signal - centre
    spread = lax.optimization_barrier(jnp.mean(centred * centred, axis=-1, keepdims=True))
    return centred * lax.rsqrt(spread + EPSILON)

def attend(queries, keys_in, values_in, allowed):
    rows_q = queries.shape[0]
    rows_k = keys_in.shape[0]
    heads_q = queries.reshape(rows_q, HEADS, HEAD)
    heads_k = keys_in.reshape(rows_k, HEADS, HEAD)
    heads_v = values_in.reshape(rows_k, HEADS, HEAD)
    scores = low_back(jnp.einsum('qhd,khd->hqk', heads_q, heads_k, precision=lax.Precision.HIGHEST) * HEAD ** (-0.5))
    scores = jnp.where(allowed[None, None, :], scores, MASKED)
    weights = low(jax.nn.softmax(scores, axis=-1))
    mixed = jnp.einsum('hqk,khd->qhd', weights, heads_v, precision=lax.Precision.HIGHEST)
    return low_back(low(mixed.reshape(rows_q, D)))

def image_forward(lowered, image_tokens, image_words, length, embedding):
    w_ada, w_qkv, w_out, w_cq, w_ckv, w_cout, w_up, w_down = lowered
    modulation = matmul(low(jax.nn.silu(embedding))[None, :], w_ada)[0]
    shift_a, scale_a, gate_a, shift_m, scale_m, gate_m = jnp.split(modulation, 6)
    hidden_a = low(layer_norm(image_tokens) * (1.0 + scale_a) + shift_a)
    projected = low_back(low(matmul(hidden_a, w_qkv)))
    every_key = jnp.arange(SEQ) >= 0
    mixed_a = attend(projected[:, :D], projected[:, D:2 * D], projected[:, 2 * D:], every_key)
    after_a = image_tokens + gate_a * low_back(matmul(mixed_a, w_out))
    hidden_c = low(layer_norm(after_a))
    cross_q = low_back(low(matmul(hidden_c, w_cq)))
    cross_kv = low_back(low(matmul(image_words, w_ckv)))
    live = jnp.arange(TLEN) < length
    mixed_c = attend(cross_q, cross_kv[:, :D], cross_kv[:, D:], live)
    after_c = after_a + low_back(matmul(mixed_c, w_cout))
    hidden_m = low(layer_norm(after_c) * (1.0 + scale_m) + shift_m)
    upward = low_back(matmul(hidden_m, w_up))
    active = low(jax.nn.gelu(upward))
    return after_c + gate_m * low_back(matmul(active, w_down))

def orthogonal(matrix):
    flipped = matrix.shape[0] > matrix.shape[1]
    work = matrix.T if flipped else matrix
    magnitude = jnp.sqrt(jnp.sum(work * work)) + 1e-07
    iterate = work / magnitude
    for turn in range(NEWTON_STEPS):
        square = matmul(iterate, iterate.T)
        quartic = matmul(square, square)
        poly = COEF_B * square + COEF_C * quartic
        iterate = COEF_A * iterate + matmul(poly, iterate)
    result = iterate.T if flipped else iterate
    return result

def reference(tokens, captions, caption_len, timestep, time_table, cotangent, w_ada, w_qkv, w_out, w_cq, w_ckv, w_cout, w_up, w_down, m_ada, m_qkv, m_out, m_cq, m_ckv, m_cout, m_up, m_down):
    masters = (w_ada, w_qkv, w_out, w_cq, w_ckv, w_cout, w_up, w_down)
    momenta = (m_ada, m_qkv, m_out, m_cq, m_ckv, m_cout, m_up, m_down)
    embedded = time_table[timestep]

    def forward(weights_in, tokens_in, words_in):
        lowered = tuple((low(matrix) for matrix in weights_in))
        checked = jax.checkpoint(image_forward)

        def advance(carry, item):
            image_tokens, image_words, length, embedding = item
            return (carry, checked(lowered, image_tokens, image_words, length, embedding))
        unused, stacked = lax.scan(advance, jnp.zeros((), jnp.float32), (tokens_in, words_in, caption_len, embedded))
        return stacked
    result, pullback = jax.vjp(forward, masters, tokens.astype(jnp.float32), captions.astype(jnp.float32))
    grads, grad_tokens, grad_captions = pullback(cotangent.astype(jnp.float32))
    fresh = tuple((DECAY * moment + grad for moment, grad in zip(momenta, grads)))
    renewed = tuple((master - RATE * math.sqrt(max(master.shape) / master.shape[0]) * orthogonal(moment) for master, moment in zip(masters, fresh)))
    return (result.astype(jnp.bfloat16), grad_tokens, grad_captions, fresh[0], fresh[1], fresh[2], fresh[3], fresh[4], fresh[5], fresh[6], fresh[7], renewed[0], renewed[1], renewed[2], renewed[3], renewed[4], renewed[5], renewed[6], renewed[7])
```

```python
import math

import jax
import jax.numpy as jnp
from jax import lax
from jax.sharding import Mesh
from jax.sharding import PartitionSpec as P

D = 512
HEADS = 8
HEAD = 64

EPSILON = 1e-06
MASKED = -1e30
RATE = 1.0
DECAY = 0.5
COEF_A = 3.4445
COEF_B = -4.775
COEF_C = 2.0315

BF16 = jnp.bfloat16
F32 = jnp.float32
WIDE = ("z", "yh", "x", "c")
SHAPES = {
    "ada": (512, 3072),
    "qkv": (512, 1536),
    "out": (512, 512),
    "cq": (512, 512),
    "ckv": (768, 1024),
    "cout": (512, 512),
    "up": (512, 2048),
    "down": (2048, 512),
}
NAMES = tuple(SHAPES)
REDUCED = ("qkv", "out", "cq", "ckv", "cout", "up", "down")


def units_of(name):
    rows, cols = SHAPES[name]
    return rows * cols // (64 * 512)


def to_units(shard):
    rows, cols = shard.shape
    blocks = shard.reshape(rows, cols // 512, 512).transpose(1, 0, 2)
    return blocks.reshape(rows * cols // 512, 512)


def from_units(stacked, rows, cols):
    count = stacked.shape[0]
    blocks = stacked.reshape(count, cols // 512, rows, 512).transpose(0, 2, 1, 3)
    return blocks.reshape(count * rows, cols)


def swap(value, axis):
    return lax.ppermute(value, axis, [(0, 1), (1, 0)])


def ordered_pair(own, other, axis, dim):
    first = lax.axis_index(axis) == 0
    return jnp.stack([jnp.where(first, own, other), jnp.where(first, other, own)], axis=dim)


def spread_to(value, axes, count):
    return lax.all_to_all(
        jnp.broadcast_to(value[None], (count,) + value.shape), axes, split_axis=0, concat_axis=0, tiled=True
    )


def layer_norm(signal):
    centre = jnp.mean(signal, axis=-1, keepdims=True)
    centred = signal - centre
    spread = jnp.mean(centred * centred, axis=-1, keepdims=True)
    return centred * lax.rsqrt(spread + EPSILON)


def norm_back(signal, upstream):
    unused, pullback = jax.vjp(layer_norm, signal)
    return pullback(upstream)[0]


def mm(left, right):
    return jnp.dot(left, right, preferred_element_type=F32)


def mm_t(left, right):
    return lax.dot_general(left, right, (((1,), (1,)), ((), ())), preferred_element_type=F32)


def t_mm(left, right):
    return lax.dot_general(left, right, (((0,), (0,)), ((), ())), preferred_element_type=F32)


def heads_of(signal):
    return signal.reshape(signal.shape[0], HEADS, HEAD)


def einsum(form, left, right):
    return jnp.einsum(form, left, right, preferred_element_type=F32)


def attend(queries, keys, values, allowed):
    scores = einsum("qhd,khd->hqk", heads_of(queries), heads_of(keys)) * HEAD ** (-0.5)
    if allowed is not None:
        scores = jnp.where(allowed, scores, MASKED)
    row_max = jnp.max(scores, axis=-1, keepdims=True)
    raised = jnp.exp(scores - row_max)
    probs = raised / jnp.sum(raised, axis=-1, keepdims=True)
    mixed = einsum("hqk,khd->qhd", probs.astype(BF16), heads_of(values))
    return mixed.reshape(queries.shape).astype(BF16), probs


def attend_back(queries, keys, values, probs, upstream):
    weights = probs.astype(BF16)
    grad_probs = einsum("qhd,khd->hqk", heads_of(upstream), heads_of(values))
    grad_values = einsum("hqk,qhd->khd", weights, heads_of(upstream))
    inner = jnp.sum(probs * grad_probs, axis=-1, keepdims=True)
    grad_scores = (probs * (grad_probs - inner)).astype(BF16)
    grad_queries = einsum("hqk,khd->qhd", grad_scores, heads_of(keys)) * HEAD ** (-0.5)
    grad_keys = einsum("hqk,qhd->khd", grad_scores, heads_of(queries)) * HEAD ** (-0.5)
    return (
        grad_queries.reshape(queries.shape).astype(BF16),
        grad_keys.reshape(keys.shape).astype(BF16),
        grad_values.reshape(keys.shape).astype(BF16),
    )


def low_dot(left, right):
    return jnp.dot(left.astype(BF16), right.astype(BF16), preferred_element_type=F32)


def high_dot(left, right):
    return jnp.dot(left, right, precision=lax.Precision.HIGH, preferred_element_type=F32)


def orthogonal_rows(matrix, pick):
    magnitude = jnp.sqrt(jnp.sum(matrix * matrix)) + 1e-07
    iterate = matrix / magnitude
    for turn in range(5):
        dot = low_dot if turn < 3 else high_dot
        square = dot(iterate, iterate.T)
        poly = COEF_B * square + COEF_C * dot(square, square)
        if turn < 4:
            iterate = COEF_A * iterate + dot(poly, iterate)
    return pick(poly, iterate)


def body(
    tokens,
    captions,
    caption_len,
    timestep,
    time_table,
    cotangent,
    *weights,
):
    masters = dict(zip(NAMES, weights[:8]))
    momenta = dict(zip(NAMES, weights[8:]))
    half = lax.axis_index("yl")
    core = lax.axis_index("c")
    low = {name: to_units(masters[name].astype(BF16)) for name in NAMES}

    def one_image(pair):
        return lax.dynamic_index_in_dim(pair, half, 0, keepdims=False)

    def other_image(pair):
        return lax.dynamic_index_in_dim(pair, 1 - half, 0, keepdims=False)

    both = jnp.stack([tokens, cotangent], axis=1)
    arrived = swap(other_image(both), "yl")
    whole = ordered_pair(one_image(both), arrived, "yl", 1).reshape(2, 256, D)
    words = one_image(captions)
    length = lax.dynamic_index_in_dim(caption_len, half, 0, keepdims=False)
    step = lax.dynamic_index_in_dim(timestep, half, 0, keepdims=False)
    embedded = lax.dynamic_slice_in_dim(time_table, step, 1, 0)
    time_gate = jax.nn.silu(embedded).astype(BF16)

    ada = low["ada"].reshape(6, 8, 512)
    early = jnp.concatenate([low["qkv"], ada[0], ada[1]], axis=0)
    middle = jnp.concatenate([low["out"], low["cq"], low["ckv"], low["cout"], ada[2]], axis=0)
    late = jnp.concatenate([low["up"], low["down"], ada[3], ada[4], ada[5]], axis=0)
    late_own = lax.all_gather(late, ("z", "yh", "x"), axis=0, tiled=False)
    early_own = spread_to(early, ("z", "yh", "x"), 32)
    early_all = ordered_pair(early_own, swap(early_own, "c"), "c", 1).reshape(64, -1, 512)
    full_qkv = from_units(early_all[:, :24], 8, 1536)
    full_ada_first = from_units(early_all[:, 24:], 8, 1024)

    modulation_first = mm(time_gate, full_ada_first)
    shift_a, scale_a = modulation_first[:, :D], modulation_first[:, D:]
    inputs = whole[0].astype(F32)
    normed_a = layer_norm(inputs)
    hidden_a = (normed_a * (1.0 + scale_a) + shift_a).astype(BF16)
    projected = mm(hidden_a, full_qkv).astype(BF16)
    queries, keys, values = projected[:, :D], projected[:, D : 2 * D], projected[:, 2 * D :]
    mixed_a, probs_a = attend(queries, keys, values, None)

    middle_own = spread_to(middle, ("z", "yh", "x"), 32)
    middle_all = ordered_pair(middle_own, swap(middle_own, "c"), "c", 1).reshape(64, -1, 512)
    full_out = from_units(middle_all[:, 0:8], 8, 512)
    full_cq = from_units(middle_all[:, 8:16], 8, 512)
    full_ckv = from_units(middle_all[:, 16:40], 12, 1024)
    full_cout = from_units(middle_all[:, 40:48], 8, 512)
    gate_a = mm(time_gate, from_units(middle_all[:, 48:56], 8, 512))

    branch_a = mm(mixed_a, full_out)
    after_a = inputs + gate_a * branch_a
    hidden_c = layer_norm(after_a).astype(BF16)
    cross_q = mm(hidden_c, full_cq).astype(BF16)
    cross_kv = mm(words, full_ckv).astype(BF16)
    live = (jnp.arange(words.shape[0]) < length)[None, None, :]
    cross_k, cross_v = cross_kv[:, :D], cross_kv[:, D:]
    mixed_c, probs_c = attend(cross_q, cross_k, cross_v, live)
    after_c = after_a + mm(mixed_c, full_cout)

    late_all = ordered_pair(late_own, swap(late_own, "c"), "c", 1).reshape(64, -1, 512)
    full_up = from_units(late_all[:, 0:32], 8, 2048)
    full_down = from_units(late_all[:, 32:64], 32, 512)
    modulation_last = mm(time_gate, from_units(late_all[:, 64:88], 8, 1536))
    shift_m, scale_m, gate_m = (
        modulation_last[:, :D],
        modulation_last[:, D : 2 * D],
        modulation_last[:, 2 * D :],
    )
    normed_m = layer_norm(after_c)
    hidden_m = (normed_m * (1.0 + scale_m) + shift_m).astype(BF16)
    upward = mm(hidden_m, full_up)
    active, gelu_pull = jax.vjp(jax.nn.gelu, upward)
    active = active.astype(BF16)
    branch_m = mm(active, full_down)
    result = (after_c + gate_m * branch_m).astype(BF16)

    grad_out = whole[1].astype(F32)
    grad_branch_m = (gate_m * grad_out).astype(BF16)
    grad_gate_m = jnp.sum(branch_m * grad_out, axis=0)
    grad_up = gelu_pull(mm_t(grad_branch_m, full_down))[0].astype(BF16)
    grad_hidden_m = mm_t(grad_up, full_up)
    grad_shift_m = jnp.sum(grad_hidden_m, axis=0)
    grad_scale_m = jnp.sum(grad_hidden_m * normed_m, axis=0)
    grad_c = grad_out + norm_back(after_c, grad_hidden_m * (1.0 + scale_m))
    grad_branch_c = grad_c.astype(BF16)
    grad_mixed_c = mm_t(grad_branch_c, full_cout).astype(BF16)
    grad_cross_q, grad_cross_k, grad_cross_v = attend_back(cross_q, cross_k, cross_v, probs_c, grad_mixed_c)
    grad_cross_kv = jnp.concatenate([grad_cross_k, grad_cross_v], axis=-1)
    grad_words = mm_t(grad_cross_kv, full_ckv)
    grad_a = grad_c + norm_back(after_a, mm_t(grad_cross_q, full_cq))
    grad_branch_a = (gate_a * grad_a).astype(BF16)
    grad_gate_a = jnp.sum(branch_a * grad_a, axis=0)
    grad_mixed_a = mm_t(grad_branch_a, full_out).astype(BF16)
    grad_q, grad_k, grad_v = attend_back(queries, keys, values, probs_a, grad_mixed_a)
    grad_projected = jnp.concatenate([grad_q, grad_k, grad_v], axis=-1)
    grad_hidden_a = mm_t(grad_projected, full_qkv)
    grad_shift_a = jnp.sum(grad_hidden_a, axis=0)
    grad_scale_a = jnp.sum(grad_hidden_a * normed_a, axis=0)
    grad_image = grad_a + norm_back(inputs, grad_hidden_a * (1.0 + scale_a))
    grad_modulation = jnp.stack(
        [grad_shift_a, grad_scale_a, grad_gate_a, grad_shift_m, grad_scale_m, grad_gate_m]
    ).astype(BF16)

    local = {
        "qkv": t_mm(hidden_a, grad_projected),
        "out": t_mm(mixed_a, grad_branch_a),
        "cq": t_mm(hidden_c, grad_cross_q),
        "ckv": t_mm(words, grad_cross_kv),
        "cout": t_mm(mixed_c, grad_branch_c),
        "up": t_mm(hidden_m, grad_up),
        "down": t_mm(active, grad_branch_m),
    }

    def core_part(name, which):
        rows, cols = SHAPES[name]
        blocks = local[name].astype(BF16).reshape(32, 2, rows // 64, cols // 512, 512)
        part = lax.dynamic_index_in_dim(blocks, which, 1, keepdims=False)
        return part.transpose(0, 2, 1, 3).reshape(32, units_of(name), 512)

    kept = jnp.concatenate([core_part(name, core) for name in REDUCED], axis=1)
    sent = jnp.concatenate([core_part(name, 1 - core) for name in REDUCED], axis=1)
    summed = (kept.astype(F32) + swap(sent, "c").astype(F32)).astype(BF16)
    riding = jnp.concatenate([grad_modulation, time_gate], axis=0)
    payload = jnp.concatenate(
        [
            summed.reshape(64, 68, 512),
            jnp.broadcast_to(riding[None], (64, 7, 512)),
        ],
        axis=1,
    )
    received = lax.all_to_all(payload, ("z", "yh", "x", "yl"), split_axis=0, concat_axis=0, tiled=True)
    mine = jnp.sum(received[:, :68].astype(F32), axis=0)
    grads = ordered_pair(mine, swap(mine, "yl"), "yl", 0).reshape(136, 512)
    images_here = received[:, 68:]
    images = jnp.concatenate([images_here, swap(images_here, "c")], axis=0)

    position = lax.axis_index(WIDE)
    gates_here = lax.dynamic_slice_in_dim(images[:, 6].T, position * 8, 8, 0)
    grad_rows = {"ada": mm(gates_here, images[:, :6].reshape(128, 3072))}
    offset = 0
    for name in REDUCED:
        rows, cols = SHAPES[name]
        size = units_of(name)
        grad_rows[name] = from_units(grads[None, offset : offset + size], rows // 64, cols)
        offset += size
    fresh = {name: DECAY * momenta[name] + grad_rows[name] for name in NAMES}

    slots = []
    for name in NAMES:
        block = to_units(fresh[name].astype(BF16))
        slots.append(jnp.pad(block, ((0, 48 - block.shape[0]), (0, 0))))
    owned = lax.all_to_all(jnp.stack(slots), ("z", "yh"), split_axis=0, concat_axis=0, tiled=True)
    owned = spread_to(owned, "x", 4)
    owned = ordered_pair(owned, swap(owned, "c"), "c", 1)
    owned = owned.transpose(2, 0, 1, 3, 4).reshape(64, 48, 512)
    group = lax.axis_index(("x", "c"))

    def branch(name):
        rows, cols = SHAPES[name]
        per = rows // 64

        def work(gathered):
            matrix = from_units(gathered[:, : units_of(name)], per, cols).astype(F32)
            if rows <= cols:

                def pick(poly, iterate):
                    def wanted(value):
                        blocks = value.reshape(8, 8, per, value.shape[-1])
                        return lax.dynamic_index_in_dim(blocks, group, 1, keepdims=False).reshape(8 * per, -1)

                    return COEF_A * wanted(iterate) + high_dot(wanted(poly), iterate)

                update = orthogonal_rows(matrix, pick)
            else:

                def pick(poly, iterate):
                    blocks = iterate.T.reshape(8, 8, per, cols)
                    wanted = lax.dynamic_index_in_dim(blocks, group, 1, keepdims=False).reshape(8 * per, cols)
                    return COEF_A * wanted + high_dot(wanted, poly)

                update = orthogonal_rows(matrix.T, pick)
            update = (RATE * math.sqrt(max(rows, cols) / rows) * update).astype(BF16)
            pieces = update.reshape(8, per, cols // 512, 512).transpose(0, 2, 1, 3)
            pieces = pieces.reshape(8, units_of(name), 512)
            return jnp.pad(pieces, ((0, 0), (0, 48 - pieces.shape[1]), (0, 0)))

        return work

    updates = lax.switch(lax.axis_index(("z", "yh")), [branch(name) for name in NAMES], owned)
    updates = lax.all_to_all(updates, ("z", "yh"), split_axis=0, concat_axis=0, tiled=True)
    renewed = {}
    for index, name in enumerate(NAMES):
        rows, cols = SHAPES[name]
        rows_here = from_units(updates[index : index + 1, : units_of(name)], rows // 64, cols)
        renewed[name] = masters[name] - rows_here.astype(F32)

    def halves(image):
        rows = image.shape[0] // 2
        parts = image.reshape(2, rows, image.shape[1])
        return ordered_pair(one_image(parts), swap(other_image(parts), "yl"), "yl", 0)

    return (
        halves(result),
        halves(grad_image),
        halves(grad_words),
        *[fresh[name] for name in NAMES],
        *[renewed[name] for name in NAMES],
    )


def solution(mesh):
    fine = Mesh(mesh.devices.reshape(4, 2, 4, 2, 2), ("z", "yh", "x", "c", "yl"))
    split = P(WIDE, "yl", None)
    rows = P(WIDE, None)
    placed = (split, P(WIDE, None, None), P(WIDE), P(WIDE), P(), split) + (rows,) * 16
    return jax.shard_map(
        body,
        mesh=fine,
        in_specs=placed,
        out_specs=(split,) * 3 + (rows,) * 16,
        check_vma=False,
    )
```

```python
import math

import jax
import jax.numpy as jnp
from jax import lax
from jax.sharding import Mesh
from jax.sharding import PartitionSpec as P

D = 512
HEADS = 8
HEAD = 64

EPSILON = 1e-06
MASKED = -1e30
RATE = 1.0
DECAY = 0.5
COEF_A = 3.4445
COEF_B = -4.775
COEF_C = 2.0315

BF16 = jnp.bfloat16
F32 = jnp.float32
WIDE = ("z", "yh", "x", "c")
SHAPES = {
    "ada": (512, 3072),
    "qkv": (512, 1536),
    "out": (512, 512),
    "cq": (512, 512),
    "ckv": (768, 1024),
    "cout": (512, 512),
    "up": (512, 2048),
    "down": (2048, 512),
}
NAMES = tuple(SHAPES)


def units_of(name):
    rows, cols = SHAPES[name]
    return rows * cols // (64 * 512)


def to_units(shard):
    rows, cols = shard.shape
    blocks = shard.reshape(rows, cols // 512, 512).transpose(1, 0, 2)
    return blocks.reshape(rows * cols // 512, 512)


def from_units(stacked, rows, cols):
    count = stacked.shape[0]
    blocks = stacked.reshape(count, cols // 512, rows, 512).transpose(0, 2, 1, 3)
    return blocks.reshape(count * rows, cols)


def eight_rows(shard):
    rows, cols = shard.shape
    blocks = -(-rows // 8)
    padded = jnp.pad(shard, ((0, 8 * blocks - rows), (0, 0)))
    return padded.reshape(blocks, 8, cols).transpose(1, 0, 2).reshape(8, blocks * cols)


def swap(value, axis):
    return lax.ppermute(value, axis, [(0, 1), (1, 0)])


def ordered_pair(own, other, axis, dim):
    first = lax.axis_index(axis) == 0
    return jnp.stack([jnp.where(first, own, other), jnp.where(first, other, own)], axis=dim)


def spread_to(value, axes, count):
    return lax.all_to_all(
        jnp.broadcast_to(value[None], (count,) + value.shape), axes, split_axis=0, concat_axis=0, tiled=True
    )


def layer_norm(signal):
    centre = jnp.mean(signal, axis=-1, keepdims=True)
    centred = signal - centre
    spread = jnp.mean(centred * centred, axis=-1, keepdims=True)
    return centred * lax.rsqrt(spread + EPSILON)


def norm_back(signal, upstream):
    unused, pullback = jax.vjp(layer_norm, signal)
    return pullback(upstream)[0]


def mm(left, right):
    return jnp.dot(left, right, preferred_element_type=F32)


def mm_t(left, right):
    return lax.dot_general(left, right, (((1,), (1,)), ((), ())), preferred_element_type=F32)


def t_mm(left, right):
    return lax.dot_general(left, right, (((0,), (0,)), ((), ())), preferred_element_type=F32)


def heads_of(signal):
    return signal.reshape(signal.shape[0], HEADS, HEAD)


def einsum(form, left, right):
    return jnp.einsum(form, left, right, preferred_element_type=F32)


def attend(queries, keys, values, allowed):
    scores = einsum("qhd,khd->hqk", heads_of(queries), heads_of(keys)) * HEAD ** (-0.5)
    if allowed is not None:
        scores = jnp.where(allowed, scores, MASKED)
    row_max = jnp.max(scores, axis=-1, keepdims=True)
    raised = jnp.exp(scores - row_max)
    probs = raised / jnp.sum(raised, axis=-1, keepdims=True)
    mixed = einsum("hqk,khd->qhd", probs.astype(BF16), heads_of(values))
    return mixed.reshape(queries.shape).astype(BF16), probs


def attend_back(queries, keys, values, probs, upstream):
    weights = probs.astype(BF16)
    grad_probs = einsum("qhd,khd->hqk", heads_of(upstream), heads_of(values))
    grad_values = einsum("hqk,qhd->khd", weights, heads_of(upstream))
    inner = jnp.sum(probs * grad_probs, axis=-1, keepdims=True)
    grad_scores = (probs * (grad_probs - inner)).astype(BF16)
    grad_queries = einsum("hqk,khd->qhd", grad_scores, heads_of(keys)) * HEAD ** (-0.5)
    grad_keys = einsum("hqk,qhd->khd", grad_scores, heads_of(queries)) * HEAD ** (-0.5)
    return (
        grad_queries.reshape(queries.shape).astype(BF16),
        grad_keys.reshape(keys.shape).astype(BF16),
        grad_values.reshape(keys.shape).astype(BF16),
    )


def low_dot(left, right):
    return mm(left.astype(BF16), right.astype(BF16))


def high_dot(left, right):
    return jnp.dot(left, right, precision=lax.Precision.HIGH, preferred_element_type=F32)


def orthogonal_poly(gram, low_turns):
    eye = jnp.eye(gram.shape[0], dtype=F32)
    inverse = 1.0 / (jnp.sqrt(jnp.sum(gram * eye)) + 1e-07)
    square = gram * (inverse * inverse)
    total = None
    for turn in range(5):
        dot = low_dot if turn < low_turns else high_dot
        poly = COEF_B * square + COEF_C * dot(square, square)
        total = COEF_A * eye + poly if total is None else COEF_A * total + dot(poly, total)
        if turn < 4:
            square = COEF_A * square + dot(poly, square)
            square = COEF_A * square + dot(poly, square)
    return total * inverse


def split_dot(left, right, form):
    high = lax.reduce_precision(left, exponent_bits=8, mantissa_bits=7)
    low = (left - high).astype(BF16)
    return einsum(form, high.astype(BF16), right) + einsum(form, low, right)


def body(
    tokens,
    captions,
    caption_len,
    timestep,
    time_table,
    cotangent,
    *weights,
):
    masters = dict(zip(NAMES, weights[:8]))
    momenta = dict(zip(NAMES, weights[8:]))
    half = lax.axis_index("yl")
    core = lax.axis_index("c")
    low = {name: to_units(masters[name].astype(BF16)) for name in NAMES}

    def one_image(pair):
        return lax.dynamic_index_in_dim(pair, half, 0, keepdims=False)

    def other_image(pair):
        return lax.dynamic_index_in_dim(pair, 1 - half, 0, keepdims=False)

    tokens_other = swap(other_image(tokens), "yl")
    words = one_image(captions)
    spot = jnp.arange(768)
    spot = spot // 12 * 16 + spot % 12
    place = (spot[:, None] == jnp.arange(1024)[None, :]).astype(BF16)
    padded_words = mm(words, place).astype(BF16)
    length = lax.dynamic_index_in_dim(caption_len, half, 0, keepdims=False)
    step = lax.dynamic_index_in_dim(timestep, half, 0, keepdims=False)
    embedded = lax.dynamic_slice_in_dim(time_table, step, 1, 0)
    time_gate = jax.nn.silu(embedded).astype(BF16)

    ada = low["ada"]
    ckv = jnp.pad(masters["ckv"], ((0, 4), (0, 0))).reshape(2, 8, 2, 512).transpose(0, 2, 1, 3)
    ckv = ckv.reshape(32, 512).astype(BF16)
    early = jnp.concatenate([low["qkv"], ada[:16]], axis=0)
    middle = jnp.concatenate([low["out"], low["cq"], ckv, low["cout"], ada[16:24]], axis=0)
    late = jnp.concatenate([low["up"], low["down"], ada[24:]], axis=0)
    late_all = lax.all_gather(late, WIDE, axis=0, tiled=True).reshape(64, 88, 512)
    early_own = spread_to(early, ("z", "yh", "x"), 32)
    early_other = swap(early_own, "c")
    middle = jnp.broadcast_to(middle[None], (32,) + middle.shape)
    cotangent_other = swap(other_image(cotangent), "yl")
    early_other, middle, cotangent_other, tokens_other = lax.optimization_barrier(
        (early_other, middle, cotangent_other, tokens_other)
    )
    image = ordered_pair(one_image(tokens), tokens_other, "yl", 0).reshape(256, D)
    early_all = ordered_pair(early_own, early_other, "c", 1).reshape(64, -1, 512)
    full_qkv = from_units(early_all[:, :24], 8, 1536)
    full_ada_first = from_units(early_all[:, 24:], 8, 1024)

    momentum_rows = jnp.concatenate([eight_rows(momenta[name]) for name in NAMES], axis=1)
    momentum_swapped = swap(momentum_rows, "c")

    modulation_first = mm(time_gate, full_ada_first)
    shift_a, scale_a = modulation_first[:, :D], modulation_first[:, D:]
    inputs = image.astype(F32)
    normed_a = layer_norm(inputs)
    hidden_a = (normed_a * (1.0 + scale_a) + shift_a).astype(BF16)
    projected = mm(hidden_a, full_qkv).astype(BF16)
    queries, keys, values = projected[:, :D], projected[:, D : 2 * D], projected[:, 2 * D :]
    mixed_a, probs_a = attend(queries, keys, values, None)

    middle_own = lax.all_to_all(middle, ("z", "yh", "x"), split_axis=0, concat_axis=0, tiled=True)
    middle_own, mixed_a, momentum_swapped = lax.optimization_barrier((middle_own, mixed_a, momentum_swapped))
    middle_all = ordered_pair(middle_own, swap(middle_own, "c"), "c", 1).reshape(64, -1, 512)
    full_out = from_units(middle_all[:, 0:8], 8, 512)
    full_cq = from_units(middle_all[:, 8:16], 8, 512)
    full_ckv = middle_all[:, 16:48].reshape(64, 2, 2, 8, 512).transpose(0, 1, 3, 2, 4).reshape(1024, 1024)
    full_cout = from_units(middle_all[:, 48:56], 8, 512)
    gate_a = mm(time_gate, from_units(middle_all[:, 56:64], 8, 512))

    branch_a = mm(mixed_a, full_out)
    after_a = inputs + gate_a * branch_a
    hidden_c = layer_norm(after_a).astype(BF16)
    cross_q = mm(hidden_c, full_cq).astype(BF16)
    cross_kv = mm(padded_words, full_ckv).astype(BF16)
    live = (jnp.arange(words.shape[0]) < length)[None, None, :]
    cross_k, cross_v = cross_kv[:, :D], cross_kv[:, D:]
    mixed_c, probs_c = attend(cross_q, cross_k, cross_v, live)
    late_all, mixed_c = lax.optimization_barrier((late_all, mixed_c))
    after_c = after_a + mm(mixed_c, full_cout)

    full_up = from_units(late_all[:, 0:32], 8, 2048)
    full_down = from_units(late_all[:, 32:64], 32, 512)
    modulation_last = mm(time_gate, from_units(late_all[:, 64:88], 8, 1536))
    shift_m, scale_m, gate_m = (
        modulation_last[:, :D],
        modulation_last[:, D : 2 * D],
        modulation_last[:, 2 * D :],
    )
    normed_m = layer_norm(after_c)
    hidden_m = (normed_m * (1.0 + scale_m) + shift_m).astype(BF16)
    upward = mm(hidden_m, full_up)
    active, gelu_pull = jax.vjp(jax.nn.gelu, upward)
    active = active.astype(BF16)
    branch_m = mm(active, full_down)
    result = (after_c + gate_m * branch_m).astype(BF16)

    def pair_grad(left, right):
        width = right.shape[1] // 2
        kept = lax.dynamic_slice_in_dim(right, core * width, width, 1)
        sent = lax.dynamic_slice_in_dim(right, (1 - core) * width, width, 1)
        lefts = jnp.concatenate([left, swap(left, "c")], axis=0)
        rights = jnp.concatenate([kept, swap(sent, "c")], axis=0)
        return t_mm(lefts, rights).astype(BF16)

    def exchange(payload):
        return lax.all_to_all(payload, ("z", "yh", "x", "yl"), split_axis=0, concat_axis=0, tiled=True)

    def total_of(received):
        return jnp.sum(received.astype(F32), axis=0)

    def settle(pieces):
        width = pieces.shape[1]
        both = ordered_pair(pieces, swap(pieces, "c"), "c", 1).reshape(8, 2 * width)
        other = lax.ppermute(both, ("c", "yl"), [(1, 2), (2, 1)])
        mine = jnp.where(core == half, both, other)
        return mine[:, :width], mine[:, width:]

    grad_out = ordered_pair(one_image(cotangent), cotangent_other, "yl", 0).reshape(256, D).astype(F32)
    grad_branch_m = (gate_m * grad_out).astype(BF16)
    grad_gate_m = jnp.sum(branch_m * grad_out, axis=0)
    grad_up = gelu_pull(mm_t(grad_branch_m, full_down))[0].astype(BF16)
    grad_hidden_m = mm_t(grad_up, full_up)
    grad_shift_m = jnp.sum(grad_hidden_m, axis=0)
    grad_scale_m = jnp.sum(grad_hidden_m * normed_m, axis=0)
    grad_c = grad_out + norm_back(after_c, grad_hidden_m * (1.0 + scale_m))
    grad_branch_c = grad_c.astype(BF16)
    part_up = pair_grad(hidden_m, grad_up).reshape(64, 8, 1024)
    part_cout = pair_grad(mixed_c, grad_branch_c).reshape(64, 8, 256)
    part_down = pair_grad(active, grad_branch_m).reshape(64, 4, 8, 256).transpose(0, 2, 1, 3).reshape(64, 8, 1024)
    first_payload = jnp.concatenate([part_up, part_down, part_cout], axis=2)
    first_payload, grad_branch_c = lax.optimization_barrier((first_payload, grad_branch_c))
    first = exchange(first_payload)

    grad_mixed_c = mm_t(grad_branch_c, full_cout).astype(BF16)
    grad_cross_q, grad_cross_k, grad_cross_v = attend_back(cross_q, cross_k, cross_v, probs_c, grad_mixed_c)
    grad_cross_kv = jnp.concatenate([grad_cross_k, grad_cross_v], axis=-1)
    grad_words = jnp.dot(
        mm_t(grad_cross_kv, full_ckv), place.T.astype(F32), precision=lax.Precision.HIGHEST, preferred_element_type=F32
    )
    grad_a = grad_c + norm_back(after_a, mm_t(grad_cross_q, full_cq))
    grad_branch_a = (gate_a * grad_a).astype(BF16)
    grad_gate_a = jnp.sum(branch_a * grad_a, axis=0)
    part_cq = pair_grad(hidden_c, grad_cross_q).reshape(64, 8, 256)
    part_out = pair_grad(mixed_a, grad_branch_a).reshape(64, 8, 256)
    part_ckv = pair_grad(padded_words, grad_cross_kv).reshape(64, 2, 8, 512).transpose(0, 2, 1, 3).reshape(64, 8, 1024)
    riding = jnp.stack([grad_gate_a, grad_shift_m, grad_scale_m, grad_gate_m]).astype(BF16)
    riding = jnp.concatenate([riding, time_gate, jnp.zeros((1, 512), BF16)], axis=0).reshape(8, 384)
    grad_mixed_a = mm_t(grad_branch_a, full_out).astype(BF16)
    grad_q, grad_k, grad_v = attend_back(queries, keys, values, probs_a, grad_mixed_a)
    grad_projected = jnp.concatenate([grad_q, grad_k, grad_v], axis=-1)
    grad_hidden_a = mm_t(grad_projected, full_qkv)
    grad_shift_a = jnp.sum(grad_hidden_a, axis=0)
    grad_scale_a = jnp.sum(grad_hidden_a * normed_a, axis=0)
    grad_image = grad_a + norm_back(inputs, grad_hidden_a * (1.0 + scale_a))
    grad_modulation = jnp.stack(
        [grad_shift_a, grad_scale_a, grad_gate_a, grad_shift_m, grad_scale_m, grad_gate_m]
    ).astype(BF16)

    part_qkv = pair_grad(hidden_a, grad_projected).reshape(64, 8, 768)
    last_riding = jnp.stack([grad_shift_a, grad_scale_a]).astype(BF16).reshape(8, 128)
    riding = jnp.concatenate([riding, last_riding], axis=1)
    second_payload = jnp.concatenate(
        [part_cq, part_out, part_ckv, part_qkv, jnp.broadcast_to(riding[None], (64, 8, 512))], axis=2
    )
    second_payload, first = lax.optimization_barrier((second_payload, first))
    second = exchange(second_payload)

    sum_1, sum_2 = total_of(first), total_of(second[..., :2304])
    sum_3 = sum_2[:, 1536:]
    sum_2 = sum_2[:, :1536]

    images = second[..., 2304:]
    images = jnp.concatenate([images, swap(images, "c")], axis=0)
    images_2 = images[..., :384].reshape(128, 3072)
    images_3 = images[..., 384:].reshape(128, 1024)
    all_grads = jnp.concatenate([images_3, images_2[:, :2048]], axis=1)
    all_gates = images_2[:, 2048:2560].T

    def gates_of(position):
        return lax.dynamic_slice_in_dim(all_gates, position * 8, 8, 0)

    momentum_rows = DECAY * jnp.where(core == half, momentum_rows, momentum_swapped)
    starts = {}
    start = 0
    for name in NAMES:
        starts[name] = start
        start += -(-SHAPES[name][0] // 512) * SHAPES[name][1]

    def momentum_piece(name):
        blocks, cols = -(-SHAPES[name][0] // 512), SHAPES[name][1]
        mine = momentum_rows[:, starts[name] : starts[name] + blocks * cols].reshape(8, blocks, cols)
        return lax.dynamic_slice_in_dim(mine, core * (cols // 2), cols // 2, 2).reshape(8, blocks * cols // 2)

    def slot(value):
        return jnp.pad(value.astype(BF16), ((0, 0), (0, 1536 - value.shape[1])))

    ada_piece = mm(gates_of(lax.axis_index(("z", "yh", "x", "yl"))), lax.dynamic_slice_in_dim(all_grads, core * 1536, 1536, 1))
    slots = jnp.stack(
        [
            slot(momentum_piece("ada") + ada_piece),
            slot(momentum_piece("qkv") + sum_3),
            slot(momentum_piece("out") + sum_2[:, 256:512]),
            slot(momentum_piece("cq") + sum_2[:, :256]),
            slot(momentum_piece("ckv") + sum_2[:, 512:]),
            slot(momentum_piece("cout") + sum_1[:, 2048:]),
            slot(momentum_piece("up") + sum_1[:, :1024]),
            slot(momentum_piece("down") + sum_1[:, 1024:2048]),
        ]
    )
    slots = jnp.broadcast_to(slots.reshape(4, 2, 1, 1, 8, 1536), (4, 2, 4, 2, 8, 1536)).reshape(64, 8, 1536)
    owned = exchange(slots)
    owned_other = swap(owned, "c")

    left_1, right_1 = settle(sum_1)
    left_2, right_2 = settle(sum_2)
    left_3, right_3 = settle(sum_3)

    def columns(left, right, start, width):
        return jnp.concatenate([left[:, start : start + width], right[:, start : start + width]], axis=1)

    def down_sums(value):
        return value[:, 1024:2048].reshape(8, 4, 256).transpose(1, 0, 2).reshape(32, 256)

    def ckv_half(value):
        return value[:, 512:1536].reshape(8, 2, 512).transpose(1, 0, 2).reshape(16, 512)[:12]

    grad_rows = {
        "ada": mm(gates_of(lax.axis_index(WIDE)), all_grads),
        "qkv": columns(left_3, right_3, 0, 768),
        "out": columns(left_2, right_2, 256, 256),
        "cq": columns(left_2, right_2, 0, 256),
        "ckv": jnp.concatenate([ckv_half(left_2), ckv_half(right_2)], axis=1),
        "cout": columns(left_1, right_1, 2048, 256),
        "up": columns(left_1, right_1, 0, 1024),
        "down": jnp.concatenate([down_sums(left_1), down_sums(right_1)], axis=1),
    }
    fresh = {name: DECAY * momenta[name] + grad_rows[name] for name in NAMES}

    group = lax.axis_index(("x", "c"))
    owner = lax.axis_index(("z", "yh"))
    is_ckv = owner == NAMES.index("ckv")
    is_down = owner == NAMES.index("down")

    def in_order(own, other):
        first = core == 0
        return jnp.concatenate([jnp.where(first, own, other), jnp.where(first, other, own)], axis=-1)

    def column_blocks(value):
        return value[..., :1024].reshape(512, 4, 256).transpose(1, 0, 2).reshape(2048, 256)

    def square_block(tops, cross, ends):
        return jnp.concatenate(
            [jnp.concatenate([tops, cross], axis=1), jnp.concatenate([cross.T, ends], axis=1)], axis=0
        )

    def ckv_rows(value):
        return jnp.concatenate(
            [value[:, :, :512].reshape(512, 512), value[:, :4, 512:1024].reshape(256, 512)], axis=0
        )

    def gram_rows(mine, others):
        mine, others = mine.reshape(512, 1536), others.reshape(512, 1536)
        return jnp.pad(mm_t(mine, mine) + mm_t(others, others), ((0, 256), (0, 256)))

    def gram_ckv(mine, others):
        mine, others = ckv_rows(mine), ckv_rows(others)
        return mm_t(mine, mine) + mm_t(others, others)

    def gram_down(mine, others):
        mine, others = column_blocks(mine), column_blocks(others)
        gram = square_block(t_mm(mine, mine), t_mm(mine, others), t_mm(others, others))
        return jnp.pad(gram, ((0, 256), (0, 256)))

    role = jnp.where(is_ckv, 1, jnp.where(is_down, 2, 0))
    poly = orthogonal_poly(lax.switch(role, [gram_rows, gram_ckv, gram_down], owned, owned_other), 3)
    poly_high = lax.reduce_precision(poly, exponent_bits=8, mantissa_bits=7)
    poly_low = (poly - poly_high).astype(BF16)
    poly_high = poly_high.astype(BF16)

    def two_terms(wanted, matrix):
        update = mm(wanted, matrix)
        count = update.shape[0] // 2
        return update[:count] + update[count:]

    def rows_of(wanted_rows):
        chosen = (wanted_rows[:, None] == jnp.arange(768)[None, :]).astype(BF16)
        return jnp.concatenate([mm(chosen, poly_high), mm(chosen, poly_low)], axis=0).astype(BF16)

    spot = jnp.arange(64)
    tops_spot = spot // 8 * 64 + group * 8 + spot % 8
    spot = jnp.arange(32)
    ends_spot = 512 + spot // 4 * 32 + group * 4 + spot % 4

    def update_rows(mine, others):
        wanted = rows_of(tops_spot)[:, :512]
        return tuple(two_terms(wanted, value.reshape(512, 1536)).reshape(8, 8, 1536).astype(BF16) for value in (mine, others))

    def update_ckv(mine, others):
        wanted = rows_of(jnp.concatenate([tops_spot, ends_spot]))

        def half_update(value):
            update = two_terms(wanted, ckv_rows(value)).astype(BF16)
            below = jnp.pad(update[64:].reshape(8, 4, 512), ((0, 0), (0, 4), (0, 0)))
            update = jnp.concatenate([update[:64].reshape(8, 8, 512), below], axis=-1)
            return jnp.pad(update, ((0, 0), (0, 0), (0, 512)))

        return half_update(mine), half_update(others)

    def update_down(mine, others):
        def group_blocks(value):
            blocks = value[..., :1024].reshape(8, 8, 8, 4, 256)
            blocks = lax.dynamic_index_in_dim(blocks, group, 1, keepdims=False)
            return blocks.transpose(2, 0, 1, 3).reshape(256, 256)

        picked = jnp.concatenate([group_blocks(mine), group_blocks(others)], axis=1)
        update = (mm(picked, poly_high[:512, :512]) + mm(picked, poly_low[:512, :512])).astype(BF16)

        def half_update(value):
            value = value.reshape(4, 8, 8, 256).transpose(1, 2, 0, 3).reshape(8, 8, 1024)
            return jnp.pad(value, ((0, 0), (0, 0), (0, 512)))

        return half_update(update[:, :256]), half_update(update[:, 256:])

    updates = in_order(*lax.switch(role, [update_rows, update_ckv, update_down], owned, owned_other))
    updates = lax.all_to_all(updates, ("z", "yh"), split_axis=0, concat_axis=0, tiled=True)
    renewed = {}
    for index, name in enumerate(NAMES):
        rows, cols = SHAPES[name]
        per = rows // 64
        width = cols // 2
        blocks = -(-per // 8)
        parts = [updates[index, :, at : at + blocks * width].reshape(8, blocks, width) for at in (0, 1536)]
        rows_here = jnp.concatenate(parts, axis=2).transpose(1, 0, 2).reshape(8 * blocks, cols)[:per]
        scale = RATE * math.sqrt(max(rows, cols) / rows)
        renewed[name] = masters[name] - scale * rows_here.astype(F32)

    def halves(image):
        rows = image.shape[0] // 2
        parts = image.reshape(2, rows, image.shape[1])
        return ordered_pair(one_image(parts), swap(other_image(parts), "yl"), "yl", 0)

    return (
        halves(result),
        halves(grad_image),
        halves(grad_words),
        *[fresh[name] for name in NAMES],
        *[renewed[name] for name in NAMES],
    )


def solution(mesh):
    fine = Mesh(mesh.devices.reshape(4, 2, 4, 2, 2), ("z", "yh", "x", "c", "yl"))
    split = P(WIDE, "yl", None)
    rows = P(WIDE, None)
    placed = (split, P(WIDE, None, None), P(WIDE), P(WIDE), P(), split) + (rows,) * 16
    return jax.shard_map(
        body,
        mesh=fine,
        in_specs=placed,
        out_specs=(split,) * 3 + (rows,) * 16,
        check_vma=False,
    )
```
